1024 devices in a mesh: dp: 128 (over x, z_hi, y, core), tensor: 8 (over z_lo).
Axes of the slice: x: 4, y: 4, z: 32 (z_hi: 4, z_lo: 8; z = z_hi * 8 + z_lo), core: 2. Of those that a mesh axis runs over, the one named last changes fastest.
Arguments:
- image_emb: bfloat16 [131072, 1152], P('dp', 'tensor'), may hold values from -0.19921875 to 0.19921875
- text_emb: bfloat16 [131072, 1152], P(('dp', 'tensor')), may hold values from -0.19921875 to 0.19921875
- partner: int32 [131072], P('dp'), may hold values from 0 to 131071, as said below
- log_scale: float32 [1], replicated, may hold values from 2 to 2.8
- logit_bias: float32 [1], replicated, may hold values from -7 to -5
Outputs:
- image_grad: bfloat16 [131072, 1152], P(('dp', 'tensor'))
- text_grad: bfloat16 [131072, 1152], P(('dp', 'tensor'))
- text_loss: float32 [131072], P(('dp', 'tensor'))
The draws below stay inside these ranges and needn't reach their ends.
Inputs may be any that keep to these rules, and one draw needn't show every extreme that they name: `partner`: every image row in block b names a text row of the same block b, and within each block every text row is named by exactly one image row.
All inputs are finite; a program needn't handle non-finite values.
Results may differ from the reference program's by a relative error of at most 0.017.
Values may be sent and summed in bfloat16 or wider, within the bound.
A program may use at most 32 MiB of HBM per device.

```python
import jax
import jax.numpy as jnp
from jax import lax

P_SIZE = 1152
ROWS = 1024
STEPS = 4
BATCH = 131072
N_DP = 128
N_TENSOR = 8


def draw_partner(key, part):
    key = jax.random.fold_in(key, 7)
    block_count = BATCH // ROWS
    block_keys = jax.random.split(key, block_count)
    orders = jax.vmap(lambda single: jax.random.permutation(single, ROWS))(block_keys)
    offsets = (jnp.arange(block_count, dtype=jnp.int32) * ROWS)[:, None]
    return (orders.astype(jnp.int32) + offsets).reshape(-1).astype(jnp.int32)


def steps_of(rng, extent, cuts, smallest, top_value):
    level = 1.0
    for dim, blocks in cuts:
        heights = jax.random.uniform(jax.random.fold_in(jax.random.fold_in(rng, 6), dim), (blocks,), jnp.float32, smallest / len(cuts), top_value / len(cuts))
        level = level * jnp.repeat(jnp.exp(heights), extent[dim] // blocks).reshape((-1,) + (1,) * (len(extent) - 1 - dim))
    return level


def noise(stream_key, dims, deviation, most, cuts=(), held_as=jnp.bfloat16):
    gain = steps_of(stream_key, dims, cuts, -0.22, 0.18) if cuts else 1.0
    result = jax.random.normal(stream_key, dims, jnp.float32) * deviation * gain
    return jnp.minimum(jnp.maximum(result, -most), most).astype(held_as)


def setup_inputs(seed: int = 0) -> dict:
    splits = jax.random.split(jax.random.key(seed), 6)
    image_emb = noise(splits[0], (BATCH, P_SIZE), 0.03, 0.19921875, ((0, 128), (1, 8)))
    text_emb = noise(splits[1], (BATCH, P_SIZE), 0.03, 0.19921875, ((0, 1024),))
    partner = draw_partner(jax.random.fold_in(splits[5], 71), 0)
    log_scale = jnp.clip(jax.random.uniform(splits[3], (1,), jnp.float32, 2.0, 2.8), 2.0, 2.8)
    logit_bias = jnp.clip(jax.random.uniform(splits[4], (1,), jnp.float32, -7.0, -5.0), -7.0, -5.0)
    return {"image_emb": image_emb, "text_emb": text_emb, "partner": partner, "log_scale": log_scale, "logit_bias": logit_bias}


epsilon = 1e-06

def unit_rows(raw):
    values = raw.astype(jnp.float32)
    scales = lax.rsqrt(lax.optimization_barrier(jnp.sum(values * values, axis=-1, keepdims=True)) + epsilon)
    return (values * scales, scales)

def normal_back(delta, units, scales):
    return scales * (delta - units * lax.optimization_barrier(jnp.sum(units * delta, axis=-1, keepdims=True)))

def reference(image_emb, text_emb, partner, log_scale, logit_bias):
    temper = jnp.exp(log_scale[0])
    offset_bias = logit_bias[0]
    share_rows = ROWS // N_TENSOR
    text_units, text_scales = unit_rows(text_emb)
    text_low = text_units.astype(jnp.bfloat16)

    def one_block(carry, index):
        delta_all, loss_all = carry
        start_img = (index * ROWS).astype(jnp.int32)
        raw = lax.dynamic_slice_in_dim(image_emb, start_img, ROWS, 0)
        image_units, image_scales = unit_rows(raw)
        image_low = image_units.astype(jnp.bfloat16)
        pairs = lax.dynamic_slice_in_dim(partner, start_img, ROWS, 0)
        parts = jnp.zeros((N_TENSOR, ROWS, P_SIZE), jnp.float32)
        for step in range(STEPS):
            owner = ((index - step) % N_DP).astype(jnp.int32)
            start_txt = (owner * ROWS).astype(jnp.int32)
            block_low = lax.dynamic_slice_in_dim(text_low, start_txt, ROWS, 0)
            columns = start_txt + jnp.arange(ROWS, dtype=jnp.int32)
            logits = temper * lax.dot_general(image_low, block_low, (((1,), (1,)), ((), ())), preferred_element_type=jnp.float32) + offset_bias
            labels = jnp.where(pairs[:, None] == columns[None, :], 1.0, -1.0).astype(jnp.float32)
            loss_cols = lax.optimization_barrier(jnp.sum(jax.nn.softplus(-labels * logits), axis=0))
            old_loss = lax.dynamic_slice_in_dim(loss_all, start_txt, ROWS, 0)
            loss_all = lax.dynamic_update_slice_in_dim(loss_all, old_loss + loss_cols, start_txt, 0)
            grad_tile = (-labels * jax.nn.sigmoid(-labels * logits)).astype(jnp.bfloat16)
            delta = temper * lax.dot_general(grad_tile, image_low, (((0,), (0,)), ((), ())), preferred_element_type=jnp.float32)
            old_delta = lax.dynamic_slice_in_dim(delta_all, start_txt, ROWS, 0)
            delta_all = lax.dynamic_update_slice_in_dim(delta_all, old_delta + delta, start_txt, 0)
            grouped = grad_tile.reshape(ROWS, N_TENSOR, share_rows).astype(jnp.float32)
            text_group = block_low.reshape(N_TENSOR, share_rows, P_SIZE).astype(jnp.float32)
            parts = parts + temper * jnp.einsum('rts,tsp->trp', grouped, text_group)
        pieces = normal_back(parts, image_units[None], image_scales[None]).astype(jnp.bfloat16)
        pieces = lax.optimization_barrier(pieces)
        block_grad = lax.optimization_barrier(jnp.sum(pieces.astype(jnp.float32), axis=0)).astype(jnp.bfloat16)
        return ((delta_all, loss_all), block_grad)
    start = (jnp.zeros((BATCH, P_SIZE), jnp.float32), jnp.zeros((BATCH,), jnp.float32))
    (delta_all, loss_all), blocks = lax.scan(one_block, start, jnp.arange(N_DP, dtype=jnp.int32))
    image_grad = blocks.reshape(BATCH, P_SIZE)
    text_grad = normal_back(delta_all, text_units, text_scales).astype(jnp.bfloat16)
    return (image_grad, text_grad, loss_all)
```

```python
import functools

import jax
import jax.numpy as jnp
from jax import lax
from jax.experimental import pallas as pl
from jax.experimental.pallas import tpu as pltpu
from jax.sharding import PartitionSpec as P

MESH = pl.DeviceIdType.MESH
epsilon = 1e-06
N_T = 8
N_DP = 128
GROUP = 8
ROWS = 1024
SHARE = ROWS // N_T
WIDTH = 1152
SLICE = WIDTH // N_T
STEPS = 4
CHUNKS = 4
LANES = ROWS // CHUNKS
PARTS = 4
WINDOW_STEPS = 46
PART = WIDTH // PARTS
STRIP = SHARE // GROUP
PAIRS = ((0, 0), (0, 1), (0, 2), (1, 0), (1, 1), (2, 0))
CARRY = WIDTH + 128
ORDER = (7, 0, 6, 1, 5, 2, 4, 3)


def kernel(
    img_ref, txt_ref, partner_ref, scale_ref, bias_ref,
    image_out, text_out, loss_out,
    images, texts, low, low_t, delta, cross, loss, piece, from_left, from_right,
    chain_out, chain_back, contrib, returned, shares,
    ag_send, ag_recv, rs_send, rs_recv, tx_send, tx_recv, spread_send, spread_recv,
    out_send, out_recv, fan_send, gr_send, gr_recv, share_send, share_recv,
    back_send, back_recv, home_send,
):
    d = lax.axis_index("dp")
    t = lax.axis_index("tensor")
    q = lax.rem(d, GROUP)
    base = d - q
    up = (jnp.where(t == N_T - 1, lax.rem(d + GROUP, N_DP), d), lax.rem(t + 1, N_T))
    down = (jnp.where(t == 0, lax.rem(d + N_DP - GROUP, N_DP), d), lax.rem(t + N_T - 1, N_T))

    def copy(src, dst, send_sem, recv_sem, where):
        return pltpu.make_async_remote_copy(
            src_ref=src, dst_ref=dst, send_sem=send_sem, recv_sem=recv_sem,
            device_id=where, device_id_type=MESH,
        )

    def arrived(view, sem):
        copy(view, view, home_send.at[0], sem, up).wait_recv()

    def left(view, sem):
        copy(view, view, sem, gr_recv.at[0], up).wait_send()

    def mate(other):
        return lax.rem(q + other, GROUP)

    def strip(p):
        return pl.ds(pl.multiple_of(p * STRIP, STRIP), STRIP)

    barrier = pltpu.get_barrier_semaphore()
    for other in range(1, GROUP):
        pl.semaphore_signal(barrier, inc=1, device_id=(base + mate(other), t), device_id_type=MESH)
    pl.semaphore_signal(barrier, inc=1, device_id=up, device_id_type=MESH)
    pl.semaphore_signal(barrier, inc=1, device_id=down, device_id_type=MESH)
    pl.semaphore_wait(barrier, GROUP - 1 + 2)

    images[t] = img_ref[...]

    def image_view(way, s, r):
        return images.at[t - s if way == 0 else t + s, :, pl.ds(r * LANES, LANES)]

    def image_copy(way, s, r):
        view = image_view(way, s, r)
        to = t + 1 if way == 0 else t - 1
        return copy(view, view, ag_send.at[way, s, r], ag_recv.at[way, s + 1, r], (d, to))

    def gather_step(pair, s, first=False):
        for r in (2 * pair, 2 * pair + 1):
            @pl.when(t >= s)
            def _():
                if not first:
                    arrived(image_view(0, s, r), ag_recv.at[0, s, r])

                @pl.when(t < N_T - 1)
                def _():
                    image_copy(0, s, r).start()

            @pl.when(t + s < N_T)
            def _():
                if not first:
                    arrived(image_view(1, s, r), ag_recv.at[1, s, r])

                @pl.when(t > 0)
                def _():
                    image_copy(1, s, r).start()

    def text_copy(k):
        return copy(txt_ref, texts.at[k], tx_send.at[k], tx_recv.at[k], (lax.rem(d + k, N_DP), t))

    def spread(b, other):
        return copy(
            txt_ref.at[strip(mate(other))], chain_out.at[0, b],
            spread_send, spread_recv, (base + mate(other), t),
        )

    for b in range(STEPS - 1):
        @pl.when(q == GROUP - 1 - b)
        def _():
            for other in range(1, GROUP):
                spread(b, other).start()
            chain_out[0, b] = txt_ref[strip(q), :]

    gather_step(0, 0, True)
    for k in range(1, STEPS):
        @pl.when(q + k < GROUP)
        def _():
            text_copy(k).start()

    def hop_out(h):
        return copy(chain_out.at[h], chain_out.at[h + 1], out_send.at[h], out_recv.at[h + 1], up)

    @pl.when(q < GROUP - 3)
    def _():
        arrived(chain_out.at[0], spread_recv)

    @pl.when(q >= GROUP - 3)
    def _():
        arrived(chain_out.at[0, pl.ds(0, 2)], spread_recv)

    hop_out(0).start()

    def first_pair(s, carry):
        gather_step(0, s)
        arrived(chain_out.at[s], out_recv.at[s])
        hop_out(s).start()
        return carry

    lax.fori_loop(1, N_T, first_pair, 0)
    gather_step(1, 0, True)
    arrived(chain_out.at[N_T], out_recv.at[N_T])

    def fan(b, e):
        k = 1 + b + e
        return copy(
            chain_out.at[N_T, b], texts.at[k, strip(q)],
            fan_send.at[b, e], tx_recv.at[k], (base + e, t),
        )

    for b, e in PAIRS:
        @pl.when(q != e)
        def _():
            fan(b, e).start()

        @pl.when(q == e)
        def _():
            texts[1 + b + e, strip(q), :] = chain_out[N_T, b]

    temper_row = jnp.exp(jnp.full((1, 128), scale_ref[0], jnp.float32))
    temper = temper_row[:, :1]
    bias = bias_ref[0]

    def text_units(k):
        raw = (txt_ref[...] if k == 0 else texts[k]).astype(jnp.float32)
        scales = lax.rsqrt(jnp.sum(raw * raw, axis=1, keepdims=True) + epsilon)
        return raw * scales, scales

    for k in range(STEPS):
        if k > 0:
            @pl.when(q >= k)
            def _():
                arrived(texts.at[k], tx_recv.at[k])

            @pl.when(q < k)
            def _():
                arrived(texts.at[k, pl.ds(0, SHARE - STRIP)], tx_recv.at[k])

        units, _ = text_units(k)
        low[pl.ds(k * SHARE, SHARE), :] = units.astype(jnp.bfloat16)
        low_t[:, pl.ds(k * SHARE, SHARE)] = units.T.astype(jnp.bfloat16)
    delta[...] = jnp.zeros_like(delta)
    cross[...] = jnp.zeros_like(cross)
    loss[...] = jnp.zeros_like(loss)

    def compute(r, carry):
        lanes = pl.ds(pl.multiple_of(r * LANES, LANES), LANES)
        raw = images[:, :, lanes].reshape(WIDTH, LANES).astype(jnp.float32)
        scales = lax.rsqrt(jnp.sum(raw * raw, axis=0, keepdims=True) + epsilon)
        unit = (raw * scales).astype(jnp.bfloat16)
        dots = jnp.dot(low[...], unit, preferred_element_type=jnp.float32)
        index = lax.broadcasted_iota(jnp.int32, (STEPS * SHARE, LANES), 0)
        step = index // SHARE
        block = d - step
        block = jnp.where(block < 0, block + N_DP, block)
        names = block * ROWS + t * SHARE + (index - step * SHARE)
        same = partner_ref[:, lanes] == names
        logits = temper * dots + bias
        z = jnp.where(same, -logits, logits)
        e = jnp.exp(z)
        u = 1.0 + e
        inverse = 1.0 / u
        sigmoid = e * inverse
        terms = jnp.log(u) + (e - (u - 1.0)) * inverse
        grad = jnp.where(same, -sigmoid, sigmoid).astype(jnp.bfloat16)
        along = grad.astype(jnp.float32) * dots
        loss[...] += terms[:, :128] + terms[:, 128:]
        cross[...] += along[:, :128] + along[:, 128:]
        delta[...] += lax.dot_general(
            grad, unit, (((1,), (1,)), ((), ())), preferred_element_type=jnp.float32
        )
        part = jnp.dot(low_t[...], grad, preferred_element_type=jnp.float32)
        back = jnp.sum(along, axis=0, keepdims=True)
        out = ((temper * scales) * (part - unit.astype(jnp.float32) * back)).astype(jnp.bfloat16)
        piece[7 - r] = out[:, :128]
        piece[r] = out[:, 128:]
        return carry

    def sum_rows(m):
        return pl.ds(pl.multiple_of(m * PART, 16), PART)

    def sum_copy(way, owner, m):
        held = from_left if way == 0 else from_right
        to = t + 1 if way == 0 else t - 1
        return copy(
            piece.at[owner, sum_rows(m)], held.at[owner, sum_rows(m)],
            rs_send.at[way, owner, m], rs_recv.at[way, owner, m], (d, to),
        )

    def sum_take(way, owner, m):
        held = from_left if way == 0 else from_right
        arrived(held.at[owner, sum_rows(m)], rs_recv.at[way, owner, m])
        total = piece[owner, sum_rows(m), :].astype(jnp.float32) + held[owner, sum_rows(m), :].astype(jnp.float32)
        piece[owner, sum_rows(m), :] = total.astype(jnp.bfloat16)

    def reduce_step(p, carry):
        for way in range(2):
            n = p - 2 * (t if way == 0 else N_T - 1 - t)

            @pl.when(jnp.logical_and(n >= 0, n < N_T * PARTS))
            def _():
                a = n // PARTS
                m = n - a * PARTS
                far = jnp.where(a % 2 == 0, N_T - 1 - a // 2, a // 2)
                owner = far if way == 0 else N_T - 1 - far

                @pl.when(owner >= t if way == 0 else owner <= t)
                def _():
                    @pl.when(t > 0 if way == 0 else t < N_T - 1)
                    def _():
                        sum_take(way, owner, m)

                    @pl.when(owner != t)
                    def _():
                        sum_copy(way, owner, m).start()

        return carry

    def second_pair(c, carry):
        gather_step(1, 2 * c + 1)
        compute(c, 0)
        gather_step(1, 2 * c + 2)
        return lax.fori_loop(4 * c, 4 * c + 4, reduce_step, carry)

    lax.fori_loop(0, 2, second_pair, 0)

    def last_slices(s, carry):
        gather_step(1, s)
        return lax.fori_loop(2 * s - 2, 2 * s, reduce_step, carry)

    lax.fori_loop(5, N_T, last_slices, 0)
    lax.fori_loop(2, 4, compute, 0)

    def text_result(k):
        rows = pl.ds(k * SHARE, SHARE)
        units, scales = text_units(k)
        back = jnp.sum(cross[rows, :], axis=1, keepdims=True)
        grads = (temper * scales) * (delta[rows, :] - units * back)
        return grads, jnp.sum(loss[rows, :], axis=1, keepdims=True)

    def grad_copy(k):
        return copy(
            contrib.at[k], returned.at[k], gr_send.at[k], gr_recv.at[k], (lax.rem(d + N_DP - k, N_DP), t)
        )

    def share_copy(k, slot, other):
        return copy(
            contrib.at[k, strip(mate(other))], shares.at[slot],
            share_send.at[k], share_recv, (base + mate(other), t),
        )

    for k in range(STEPS - 1, 0, -1):
        grads, total = text_result(k)
        contrib[k, :, pl.ds(0, WIDTH)] = grads.astype(jnp.bfloat16)
        contrib[k, :, pl.ds(WIDTH, 128)] = jnp.broadcast_to(total, (SHARE, 128)).astype(jnp.bfloat16)

        for slot, (b, e) in enumerate(PAIRS):
            if 1 + b + e == k:
                @pl.when(q == e)
                def _():
                    for other in range(1, GROUP):
                        share_copy(k, slot, other).start()
                    shares[slot] = contrib[k, strip(q), :]

        @pl.when(q >= k)
        def _():
            grad_copy(k).start()

    lax.fori_loop(14, 20, reduce_step, 0)

    def hop_back(h):
        return copy(chain_back.at[h], chain_back.at[h + 1], back_send.at[h], back_recv.at[h + 1], down)

    for e in range(STEPS - 1):
        @pl.when(q == e)
        def _():
            arrived(shares.at[pl.ds(0, STEPS - 1 + e)], share_recv)

    @pl.when(q >= STEPS - 1)
    def _():
        arrived(shares, share_recv)

    for b in range(STEPS - 1):
        total = None
        for slot, (bb, e) in enumerate(PAIRS):
            if bb == b:
                term = shares[slot].astype(jnp.float32)
                total = term if total is None else total + term
        chain_back[0, b] = total.astype(jnp.bfloat16)
    hop_back(0).start()

    def tail(h, carry):
        lax.fori_loop(17 + 3 * h, 20 + 3 * h, reduce_step, carry)
        arrived(chain_back.at[h], back_recv.at[h])
        hop_back(h).start()
        return carry

    lax.fori_loop(1, N_T, tail, 0)
    lax.fori_loop(41, WINDOW_STEPS, reduce_step, 0)
    arrived(chain_back.at[N_T], back_recv.at[N_T])

    def home(b):
        return copy(
            chain_back.at[N_T, b], returned.at[3, strip(q)],
            home_send.at[b], gr_recv.at[3], (base + GROUP - 1 - b, t),
        )

    for b in range(STEPS - 1):
        @pl.when(q != GROUP - 1 - b)
        def _():
            home(b).start()

        @pl.when(q == GROUP - 1 - b)
        def _():
            returned[3, strip(q), :] = chain_back[N_T, b]

    image_out[...] = piece[t].astype(jnp.float32).T.astype(jnp.bfloat16)

    grads, total = text_result(0)
    total = jnp.broadcast_to(total, (SHARE, 128))
    delta[pl.ds(0, SHARE), :] = grads
    loss[pl.ds(0, SHARE), :] = total

    def take(k):
        delta[pl.ds(0, SHARE), :] += returned[k, :, pl.ds(0, WIDTH)].astype(jnp.float32)
        loss[pl.ds(0, SHARE), :] += returned[k, :, pl.ds(WIDTH, 128)].astype(jnp.float32)

    for k in range(1, STEPS - 1):
        @pl.when(q + k < GROUP)
        def _():
            arrived(returned.at[k], gr_recv.at[k])
            take(k)

    @pl.when(q + 3 < GROUP)
    def _():
        arrived(returned.at[3], gr_recv.at[3])

    @pl.when(q + 3 >= GROUP)
    def _():
        arrived(returned.at[3, pl.ds(0, SHARE - STRIP)], gr_recv.at[3])

    take(3)
    text_out[...] = delta[pl.ds(0, SHARE), :].astype(jnp.bfloat16)
    loss_out[...] = loss[pl.ds(0, SHARE), :].T[:8]

    @pl.when(q >= GROUP - 3)
    def _():
        left(txt_ref.at[pl.ds(0, SHARE - STRIP)], spread_send)

    for b, e in PAIRS:
        @pl.when(q != e)
        def _():
            fan(b, e).wait_send()

    for b in range(STEPS - 1):
        @pl.when(q != GROUP - 1 - b)
        def _():
            home(b).wait_send()

    for k in range(1, STEPS):
        @pl.when(q + k < GROUP)
        def _():
            text_copy(k).wait_send()

        @pl.when(q < k)
        def _():
            left(contrib.at[k, pl.ds(0, SHARE - STRIP)], share_send.at[k])

        @pl.when(q >= k)
        def _():
            grad_copy(k).wait_send()

    def drain(s, carry):
        hop_out(s).wait_send()
        hop_back(s).wait_send()
        for r in range(CHUNKS):
            @pl.when(jnp.logical_and(t >= s, t < N_T - 1))
            def _():
                image_copy(0, s, r).wait_send()

            @pl.when(jnp.logical_and(t + s < N_T, t > 0))
            def _():
                image_copy(1, s, r).wait_send()

        for m in range(PARTS):
            @pl.when(s > t)
            def _():
                sum_copy(0, s, m).wait_send()

            @pl.when(s < t)
            def _():
                sum_copy(1, s, m).wait_send()

        return carry

    lax.fori_loop(0, N_T, drain, 0)


def local(image_emb, text_emb, partner, log_scale, logit_bias):
    by_owner = image_emb.reshape(N_T, SHARE, SLICE)
    ordered = jnp.concatenate([by_owner[o] for o in ORDER], axis=0).T
    pairs = partner.reshape(N_T, SHARE)
    pairs = jnp.concatenate([pairs[o] for o in ORDER]).reshape(1, ROWS)
    bf16, f32 = jnp.bfloat16, jnp.float32
    dma = pltpu.SemaphoreType.DMA
    vmem = pl.BlockSpec(memory_space=pltpu.VMEM)
    smem = pl.BlockSpec(memory_space=pltpu.SMEM)
    image_grad, text_grad, text_loss = pl.pallas_call(
        kernel,
        name="window_loss",
        out_shape=(
            jax.ShapeDtypeStruct((SHARE, WIDTH), bf16),
            jax.ShapeDtypeStruct((SHARE, WIDTH), bf16),
            jax.ShapeDtypeStruct((8, SHARE), f32),
        ),
        in_specs=[vmem, vmem, vmem, smem, smem],
        out_specs=(vmem, vmem, vmem),
        scratch_shapes=[
            pltpu.VMEM((N_T, SLICE, ROWS), bf16),
            pltpu.VMEM((STEPS, SHARE, WIDTH), bf16),
            pltpu.VMEM((STEPS * SHARE, WIDTH), bf16),
            pltpu.VMEM((WIDTH, STEPS * SHARE), bf16),
            pltpu.VMEM((STEPS * SHARE, WIDTH), f32),
            pltpu.VMEM((STEPS * SHARE, 128), f32),
            pltpu.VMEM((STEPS * SHARE, 128), f32),
            pltpu.VMEM((N_T, WIDTH, SHARE), bf16),
            pltpu.VMEM((N_T, WIDTH, SHARE), bf16),
            pltpu.VMEM((N_T, WIDTH, SHARE), bf16),
            pltpu.VMEM((N_T + 1, STEPS - 1, STRIP, WIDTH), bf16),
            pltpu.VMEM((N_T + 1, STEPS - 1, STRIP, CARRY), bf16),
            pltpu.VMEM((STEPS, SHARE, CARRY), bf16),
            pltpu.VMEM((STEPS, SHARE, CARRY), bf16),
            pltpu.VMEM((len(PAIRS), STRIP, CARRY), bf16),
            dma((2, N_T + 1, CHUNKS)), dma((2, N_T + 1, CHUNKS)),
            dma((2, N_T, PARTS)), dma((2, N_T, PARTS)),
            dma((STEPS,)), dma((STEPS,)), dma, dma,
            dma((N_T,)), dma((N_T + 1,)), dma((STEPS - 1, STEPS - 1)),
            dma((STEPS,)), dma((STEPS,)), dma((STEPS,)), dma,
            dma((N_T,)), dma((N_T + 1,)), dma((STEPS - 1,)),
        ],
        compiler_params=pltpu.CompilerParams(
            collective_id=0, has_side_effects=True, vmem_limit_bytes=56 * 2**20
        ),
    )(ordered, text_emb, pairs, log_scale, logit_bias)
    return image_grad, text_grad, text_loss[0]


def solution(mesh):
    placed = (P("dp", "tensor"), P(("dp", "tensor"), None), P("dp"), P(), P())
    return jax.shard_map(
        local,
        mesh=mesh,
        in_specs=placed,
        out_specs=(P(("dp", "tensor"), None), P(("dp", "tensor"), None), P(("dp", "tensor"))),
        check_vma=False,
    )
```

```python
import functools

import jax
import jax.numpy as jnp
from jax import lax
from jax.experimental import pallas as pl
from jax.experimental.pallas import tpu as pltpu
from jax.sharding import PartitionSpec as P

MESH = pl.DeviceIdType.MESH
epsilon = 1e-06
N_T = 8
N_DP = 128
GROUP = 8
ROWS = 1024
SHARE = ROWS // N_T
WIDTH = 1152
SLICE = WIDTH // N_T
STEPS = 4
CHUNKS = 4
LANES = ROWS // CHUNKS
PARTS = 4
WINDOW_STEPS = 46
PART = WIDTH // PARTS
STRIP = SHARE // GROUP
PAIRS = ((0, 0), (0, 1), (0, 2), (1, 0), (1, 1), (2, 0))
CARRY = WIDTH + 128
ORDER = (7, 0, 6, 1, 5, 2, 4, 3)


def kernel(
    img_ref, txt_ref, partner_ref, scale_ref, bias_ref,
    image_out, text_out, loss_out,
    images, texts, low, low_t, delta, cross, loss, piece, from_left, from_right,
    chain_out, chain_back, contrib, returned, shares,
    ag_send, ag_recv, rs_send, rs_recv, tx_send, tx_recv, spread_send, spread_recv,
    out_send, out_recv, fan_send, gr_send, gr_recv, share_send, share_recv,
    back_send, back_recv, home_send,
):
    d = lax.axis_index("dp")
    t = lax.axis_index("tensor")
    q = lax.rem(d, GROUP)
    base = d - q
    up = (jnp.where(t == N_T - 1, lax.rem(d + GROUP, N_DP), d), lax.rem(t + 1, N_T))
    down = (jnp.where(t == 0, lax.rem(d + N_DP - GROUP, N_DP), d), lax.rem(t + N_T - 1, N_T))

    def copy(src, dst, send_sem, recv_sem, where):
        return pltpu.make_async_remote_copy(
            src_ref=src, dst_ref=dst, send_sem=send_sem, recv_sem=recv_sem,
            device_id=where, device_id_type=MESH,
        )

    def arrived(view, sem):
        copy(view, view, home_send.at[0], sem, up).wait_recv()

    def left(view, sem):
        copy(view, view, sem, gr_recv.at[0], up).wait_send()

    def mate(other):
        return lax.rem(q + other, GROUP)

    def strip(p):
        return pl.ds(pl.multiple_of(p * STRIP, STRIP), STRIP)

    barrier = pltpu.get_barrier_semaphore()
    for other in range(1, GROUP):
        pl.semaphore_signal(barrier, inc=1, device_id=(base + mate(other), t), device_id_type=MESH)
    pl.semaphore_signal(barrier, inc=1, device_id=up, device_id_type=MESH)
    pl.semaphore_signal(barrier, inc=1, device_id=down, device_id_type=MESH)
    pl.semaphore_wait(barrier, GROUP - 1 + 2)

    for place, owner in enumerate(ORDER):
        images[t, :, pl.ds(place * SHARE, SHARE)] = img_ref[:, pl.ds(owner * SHARE, SHARE)]

    def image_view(way, s, r):
        return images.at[t - s if way == 0 else t + s, :, pl.ds(r * LANES, LANES)]

    def image_copy(way, s, r):
        view = image_view(way, s, r)
        to = t + 1 if way == 0 else t - 1
        return copy(view, view, ag_send.at[way, s], ag_recv.at[way, s + 1, r], (d, to))

    def gather_step(pair, s, first=False):
        for r in (2 * pair, 2 * pair + 1):
            @pl.when(t >= s)
            def _():
                if not first:
                    arrived(image_view(0, s, r), ag_recv.at[0, s, r])

                @pl.when(t < N_T - 1)
                def _():
                    image_copy(0, s, r).start()

            @pl.when(t + s < N_T)
            def _():
                if not first:
                    arrived(image_view(1, s, r), ag_recv.at[1, s, r])

                @pl.when(t > 0)
                def _():
                    image_copy(1, s, r).start()

    def text_copy(k):
        return copy(txt_ref, texts.at[k], tx_send.at[k], tx_recv.at[k], (lax.rem(d + k, N_DP), t))

    def spread(b, other):
        return copy(
            txt_ref.at[strip(mate(other))], chain_out.at[0, b],
            spread_send, spread_recv, (base + mate(other), t),
        )

    for b in range(STEPS - 1):
        @pl.when(q == GROUP - 1 - b)
        def _():
            for other in range(1, GROUP):
                spread(b, other).start()
            chain_out[0, b] = txt_ref[strip(q), :]

    gather_step(0, 0, True)
    for k in range(1, STEPS):
        @pl.when(q + k < GROUP)
        def _():
            text_copy(k).start()

    def hop_out(h, b):
        return copy(chain_out.at[h, b], chain_out.at[h + 1, b], out_send.at[h], out_recv.at[h + 1, b], up)

    def pass_out(h):
        for b in range(STEPS - 1):
            arrived(chain_out.at[h, b], out_recv.at[h, b])
            hop_out(h, b).start()

    @pl.when(q < GROUP - 3)
    def _():
        arrived(chain_out.at[0], spread_recv)

    @pl.when(q >= GROUP - 3)
    def _():
        arrived(chain_out.at[0, pl.ds(0, 2)], spread_recv)

    for b in range(STEPS - 1):
        hop_out(0, b).start()

    def text_units(k):
        raw = (txt_ref[...] if k == 0 else texts[k]).astype(jnp.float32)
        scales = lax.rsqrt(jnp.sum(raw * raw, axis=1, keepdims=True) + epsilon)
        return raw * scales, scales

    def text_low(k):
        units, _ = text_units(k)
        low[pl.ds(k * SHARE, SHARE), :] = units.astype(jnp.bfloat16)
        low_t[:, pl.ds(k * SHARE, SHARE)] = units.T.astype(jnp.bfloat16)

    text_low(0)
    delta[...] = jnp.zeros_like(delta)
    cross[...] = jnp.zeros_like(cross)
    loss[...] = jnp.zeros_like(loss)

    def first_pair(s, carry):
        pass_out(s)
        gather_step(0, s)
        return carry

    lax.fori_loop(1, N_T, first_pair, 0)
    gather_step(1, 0, True)

    def fan(b, e):
        k = 1 + b + e
        return copy(
            chain_out.at[N_T, b], texts.at[k, strip(q)],
            fan_send.at[b, e], tx_recv.at[k], (base + e, t),
        )

    for b, e in PAIRS:
        if e == 0:
            arrived(chain_out.at[N_T, b], out_recv.at[N_T, b])

        @pl.when(q != e)
        def _():
            fan(b, e).start()

        @pl.when(q == e)
        def _():
            texts[1 + b + e, strip(q), :] = chain_out[N_T, b]

    gather_step(1, 1)

    temper_row = jnp.exp(jnp.full((1, 128), scale_ref[0], jnp.float32))
    temper = temper_row[:, :1]
    bias = bias_ref[0]

    for k in range(1, STEPS):
        @pl.when(q >= k)
        def _():
            arrived(texts.at[k], tx_recv.at[k])

        @pl.when(q < k)
        def _():
            arrived(texts.at[k, pl.ds(0, SHARE - STRIP)], tx_recv.at[k])

        text_low(k)

    def lane_block(owner):
        return pl.ds(pl.multiple_of(owner * SHARE, SHARE), SHARE)

    def compute(r, carry):
        lanes = pl.ds(pl.multiple_of(r * LANES, LANES), LANES)
        raw = images[:, :, lanes].reshape(WIDTH, LANES).astype(jnp.float32)
        scales = lax.rsqrt(jnp.sum(raw * raw, axis=0, keepdims=True) + epsilon)
        unit = (raw * scales).astype(jnp.bfloat16)
        dots = jnp.dot(low[...], unit, preferred_element_type=jnp.float32)
        index = lax.broadcasted_iota(jnp.int32, (STEPS * SHARE, LANES), 0)
        step = index // SHARE
        block = d - step
        block = jnp.where(block < 0, block + N_DP, block)
        names = block * ROWS + t * SHARE + (index - step * SHARE)
        pairs = jnp.concatenate([partner_ref[:, lane_block(N_T - 1 - r)], partner_ref[:, lane_block(r)]], axis=1)
        same = pairs == names
        logits = temper * dots + bias
        z = jnp.where(same, -logits, logits)
        e = jnp.exp(z)
        u = 1.0 + e
        inverse = 1.0 / u
        sigmoid = e * inverse
        terms = jnp.log(u) + (e - (u - 1.0)) * inverse
        grad = jnp.where(same, -sigmoid, sigmoid).astype(jnp.bfloat16)
        along = grad.astype(jnp.float32) * dots
        loss[...] += terms[:, :128] + terms[:, 128:]
        cross[...] += along[:, :128] + along[:, 128:]
        delta[...] += lax.dot_general(
            grad, unit, (((1,), (1,)), ((), ())), preferred_element_type=jnp.float32
        )
        part = jnp.dot(low_t[...], grad, preferred_element_type=jnp.float32)
        back = jnp.sum(along, axis=0, keepdims=True)
        out = ((temper * scales) * (part - unit.astype(jnp.float32) * back)).astype(jnp.bfloat16)
        piece[7 - r] = out[:, :128]
        piece[r] = out[:, 128:]
        return carry

    def sum_rows(m):
        return pl.ds(pl.multiple_of(m * PART, 16), PART)

    def sum_copy(way, owner, m):
        held = from_left if way == 0 else from_right
        to = t + 1 if way == 0 else t - 1
        return copy(
            piece.at[owner, sum_rows(m)], held.at[owner, sum_rows(m)],
            rs_send.at[way, owner], rs_recv.at[way, owner, m], (d, to),
        )

    def sum_take(way, owner, m):
        held = from_left if way == 0 else from_right
        arrived(held.at[owner, sum_rows(m)], rs_recv.at[way, owner, m])
        total = piece[owner, sum_rows(m), :].astype(jnp.float32) + held[owner, sum_rows(m), :].astype(jnp.float32)
        piece[owner, sum_rows(m), :] = total.astype(jnp.bfloat16)

    def reduce_step(p, carry):
        for way in range(2):
            n = p - 2 * (t if way == 0 else N_T - 1 - t)

            @pl.when(jnp.logical_and(n >= 0, n < N_T * PARTS))
            def _():
                a = n // PARTS
                m = n - a * PARTS
                far = jnp.where(a % 2 == 0, N_T - 1 - a // 2, a // 2)
                owner = far if way == 0 else N_T - 1 - far

                @pl.when(owner >= t if way == 0 else owner <= t)
                def _():
                    @pl.when(t > 0 if way == 0 else t < N_T - 1)
                    def _():
                        sum_take(way, owner, m)

                    @pl.when(owner != t)
                    def _():
                        sum_copy(way, owner, m).start()

        return carry

    def second_pair(c, carry):
        compute(c, 0)
        gather_step(1, 2 * c + 2)
        lax.fori_loop(4 * c, 4 * c + 4, reduce_step, 0)
        gather_step(1, 2 * c + 3)
        return carry

    lax.fori_loop(0, 2, second_pair, 0)

    def last_slices(s, carry):
        gather_step(1, s)
        return lax.fori_loop(3 * s - 10, 3 * s - 7, reduce_step, carry)

    lax.fori_loop(6, N_T, last_slices, 0)
    compute(2, 0)
    lax.fori_loop(14, 18, reduce_step, 0)
    compute(3, 0)

    def text_result(k):
        rows = pl.ds(k * SHARE, SHARE)
        units, scales = text_units(k)
        back = jnp.sum(cross[rows, :], axis=1, keepdims=True)
        grads = (temper * scales) * (delta[rows, :] - units * back)
        return grads, jnp.sum(loss[rows, :], axis=1, keepdims=True)

    def grad_copy(k):
        return copy(
            contrib.at[k], returned.at[k], gr_send.at[k], gr_recv.at[k], (lax.rem(d + N_DP - k, N_DP), t)
        )

    def share_copy(k, slot, other):
        return copy(
            contrib.at[k, strip(mate(other))], shares.at[slot],
            share_send.at[k], share_recv, (base + mate(other), t),
        )

    for k in range(STEPS - 1, 0, -1):
        grads, total = text_result(k)
        contrib[k, :, pl.ds(0, WIDTH)] = grads.astype(jnp.bfloat16)
        contrib[k, :, pl.ds(WIDTH, 128)] = jnp.broadcast_to(total, (SHARE, 128)).astype(jnp.bfloat16)

        for slot, (b, e) in enumerate(PAIRS):
            if 1 + b + e == k:
                @pl.when(q == e)
                def _():
                    for other in range(1, GROUP):
                        share_copy(k, slot, other).start()
                    shares[slot] = contrib[k, strip(q), :]

    lax.fori_loop(18, 22, reduce_step, 0)

    def hop_back(h, b):
        return copy(
            chain_back.at[h, b], chain_back.at[h + 1, b], back_send.at[h], back_recv.at[h + 1, b], down
        )

    def pass_back(h):
        for b in range(STEPS - 1):
            arrived(chain_back.at[h, b], back_recv.at[h, b])
            hop_back(h, b).start()

    for e in range(STEPS - 1):
        @pl.when(q == e)
        def _():
            arrived(shares.at[pl.ds(0, STEPS - 1 + e)], share_recv)

    @pl.when(q >= STEPS - 1)
    def _():
        arrived(shares, share_recv)

    for b in range(STEPS - 1):
        total = None
        for slot, (bb, e) in enumerate(PAIRS):
            if bb == b:
                term = shares[slot].astype(jnp.float32)
                total = term if total is None else total + term
        chain_back[0, b] = total.astype(jnp.bfloat16)
        hop_back(0, b).start()

    for k in range(1, STEPS):
        @pl.when(q >= k)
        def _():
            grad_copy(k).start()

    grads, total = text_result(0)
    total = jnp.broadcast_to(total, (SHARE, 128))
    delta[pl.ds(0, SHARE), :] = grads
    loss[pl.ds(0, SHARE), :] = total

    def tail(h, carry):
        lax.fori_loop(20 + 2 * h, 22 + 2 * h, reduce_step, carry)
        pass_back(h)
        return carry

    lax.fori_loop(1, N_T, tail, 0)
    lax.fori_loop(36, 40, reduce_step, 0)

    def home(b):
        return copy(
            chain_back.at[N_T, b], returned.at[3, strip(q)],
            home_send.at[b], gr_recv.at[3], (base + GROUP - 1 - b, t),
        )

    for b in range(STEPS - 1):
        arrived(chain_back.at[N_T, b], back_recv.at[N_T, b])

        @pl.when(q != GROUP - 1 - b)
        def _():
            home(b).start()

        @pl.when(q == GROUP - 1 - b)
        def _():
            returned[3, strip(q), :] = chain_back[N_T, b]

    lax.fori_loop(40, WINDOW_STEPS, reduce_step, 0)
    image_out[...] = piece[t].astype(jnp.float32).T.astype(jnp.bfloat16)

    def take(k):
        delta[pl.ds(0, SHARE), :] += returned[k, :, pl.ds(0, WIDTH)].astype(jnp.float32)
        loss[pl.ds(0, SHARE), :] += returned[k, :, pl.ds(WIDTH, 128)].astype(jnp.float32)

    for k in range(1, STEPS - 1):
        @pl.when(q + k < GROUP)
        def _():
            arrived(returned.at[k], gr_recv.at[k])
            take(k)

    @pl.when(q + 3 < GROUP)
    def _():
        arrived(returned.at[3], gr_recv.at[3])

    @pl.when(q + 3 >= GROUP)
    def _():
        arrived(returned.at[3, pl.ds(0, SHARE - STRIP)], gr_recv.at[3])

    take(3)
    text_out[...] = delta[pl.ds(0, SHARE), :].astype(jnp.bfloat16)
    loss_out[...] = loss[pl.ds(0, SHARE), :].T[:1]

    @pl.when(q >= GROUP - 3)
    def _():
        left(txt_ref.at[pl.ds(0, SHARE - STRIP)], spread_send)

    for b, e in PAIRS:
        @pl.when(q != e)
        def _():
            fan(b, e).wait_send()

    for b in range(STEPS - 1):
        @pl.when(q != GROUP - 1 - b)
        def _():
            home(b).wait_send()

    for k in range(1, STEPS):
        @pl.when(q + k < GROUP)
        def _():
            text_copy(k).wait_send()

        @pl.when(q < k)
        def _():
            left(contrib.at[k, pl.ds(0, SHARE - STRIP)], share_send.at[k])

        @pl.when(q >= k)
        def _():
            grad_copy(k).wait_send()

    def drain(s, carry):
        left(chain_out.at[s], out_send.at[s])
        left(chain_back.at[s], back_send.at[s])

        @pl.when(jnp.logical_and(t >= s, t < N_T - 1))
        def _():
            left(images.at[s], ag_send.at[0, s])

        @pl.when(jnp.logical_and(t + s < N_T, t > 0))
        def _():
            left(images.at[s], ag_send.at[1, s])

        @pl.when(s > t)
        def _():
            left(piece.at[s], rs_send.at[0, s])

        @pl.when(s < t)
        def _():
            left(piece.at[s], rs_send.at[1, s])

        return carry

    lax.fori_loop(0, N_T, drain, 0)


def local(image_emb, text_emb, partner, log_scale, logit_bias):
    ordered = image_emb.T
    pairs = partner.reshape(1, ROWS)
    bf16, f32 = jnp.bfloat16, jnp.float32
    dma = pltpu.SemaphoreType.DMA
    vmem = pl.BlockSpec(memory_space=pltpu.VMEM)
    smem = pl.BlockSpec(memory_space=pltpu.SMEM)
    image_grad, text_grad, text_loss = pl.pallas_call(
        kernel,
        name="window_loss",
        out_shape=(
            jax.ShapeDtypeStruct((SHARE, WIDTH), bf16),
            jax.ShapeDtypeStruct((SHARE, WIDTH), bf16),
            jax.ShapeDtypeStruct((1, SHARE), f32),
        ),
        in_specs=[vmem, vmem, vmem, smem, smem],
        out_specs=(vmem, vmem, vmem),
        scratch_shapes=[
            pltpu.VMEM((N_T, SLICE, ROWS), bf16),
            pltpu.VMEM((STEPS, SHARE, WIDTH), bf16),
            pltpu.VMEM((STEPS * SHARE, WIDTH), bf16),
            pltpu.VMEM((WIDTH, STEPS * SHARE), bf16),
            pltpu.VMEM((STEPS * SHARE, WIDTH), f32),
            pltpu.VMEM((STEPS * SHARE, 128), f32),
            pltpu.VMEM((STEPS * SHARE, 128), f32),
            pltpu.VMEM((N_T, WIDTH, SHARE), bf16),
            pltpu.VMEM((N_T, WIDTH, SHARE), bf16),
            pltpu.VMEM((N_T, WIDTH, SHARE), bf16),
            pltpu.VMEM((N_T + 1, STEPS - 1, STRIP, WIDTH), bf16),
            pltpu.VMEM((N_T + 1, STEPS - 1, STRIP, CARRY), bf16),
            pltpu.VMEM((STEPS, SHARE, CARRY), bf16),
            pltpu.VMEM((STEPS, SHARE, CARRY), bf16),
            pltpu.VMEM((len(PAIRS), STRIP, CARRY), bf16),
            dma((2, N_T)), dma((2, N_T + 1, CHUNKS)),
            dma((2, N_T)), dma((2, N_T, PARTS)),
            dma((STEPS,)), dma((STEPS,)), dma, dma,
            dma((N_T,)), dma((N_T + 1, STEPS - 1)), dma((STEPS - 1, STEPS - 1)),
            dma((STEPS,)), dma((STEPS,)), dma((STEPS,)), dma,
            dma((N_T,)), dma((N_T + 1, STEPS - 1)), dma((STEPS - 1,)),
        ],
        compiler_params=pltpu.CompilerParams(
            collective_id=0, has_side_effects=True, vmem_limit_bytes=56 * 2**20
        ),
    )(ordered, text_emb, pairs, log_scale, logit_bias)
    return image_grad, text_grad, text_loss.reshape(SHARE)


def solution(mesh):
    placed = (P("dp", "tensor"), P(("dp", "tensor"), None), P("dp"), P(), P())
    return jax.shard_map(
        local,
        mesh=mesh,
        in_specs=placed,
        out_specs=(P(("dp", "tensor"), None), P(("dp", "tensor"), None), P(("dp", "tensor"))),
        check_vma=False,
    )
```

```python
import functools

import jax
import jax.numpy as jnp
from jax import lax
from jax.experimental import pallas as pl
from jax.experimental.pallas import tpu as pltpu
from jax.sharding import PartitionSpec as P

MESH = pl.DeviceIdType.MESH
epsilon = 1e-06
N_T = 8
N_DP = 128
GROUP = 8
ROWS = 1024
SHARE = ROWS // N_T
WIDTH = 1152
SLICE = WIDTH // N_T
STEPS = 4
CHUNKS = 4
LANES = ROWS // CHUNKS
PARTS = 4
WINDOW_STEPS = 46
PART = WIDTH // PARTS
STRIP = SHARE // GROUP
PAIRS = ((0, 0), (0, 1), (0, 2), (1, 0), (1, 1), (2, 0))
CARRY = WIDTH + 128
ORDER = (7, 0, 6, 1, 5, 2, 4, 3)


def kernel(
    img_ref, txt_ref, partner_ref, scale_ref, bias_ref,
    image_out, text_out, loss_out,
    images, texts, low, low_t, delta, cross, loss, piece, from_left, from_right,
    chain_out, chain_back, contrib, returned, shares,
    ag_send, ag_recv, rs_send, rs_recv, tx_send, tx_recv, spread_send, spread_recv,
    out_send, out_recv, fan_send, gr_send, gr_recv, share_send, share_recv,
    back_send, back_recv, home_send,
):
    d = lax.axis_index("dp")
    t = lax.axis_index("tensor")
    q = lax.rem(d, GROUP)
    base = d - q
    up = (jnp.where(t == N_T - 1, lax.rem(d + GROUP, N_DP), d), lax.rem(t + 1, N_T))
    down = (jnp.where(t == 0, lax.rem(d + N_DP - GROUP, N_DP), d), lax.rem(t + N_T - 1, N_T))

    def copy(src, dst, send_sem, recv_sem, where):
        return pltpu.make_async_remote_copy(
            src_ref=src, dst_ref=dst, send_sem=send_sem, recv_sem=recv_sem,
            device_id=where, device_id_type=MESH,
        )

    def arrived(view, sem):
        copy(view, view, home_send.at[0], sem, up).wait_recv()

    def left(view, sem):
        copy(view, view, sem, gr_recv.at[0], up).wait_send()

    def mate(other):
        return lax.rem(q + other, GROUP)

    def strip(p):
        return pl.ds(pl.multiple_of(p * STRIP, STRIP), STRIP)

    barrier = pltpu.get_barrier_semaphore()
    for other in range(1, GROUP):
        pl.semaphore_signal(barrier, inc=1, device_id=(base + mate(other), t), device_id_type=MESH)
    pl.semaphore_signal(barrier, inc=1, device_id=up, device_id_type=MESH)
    pl.semaphore_signal(barrier, inc=1, device_id=down, device_id_type=MESH)
    pl.semaphore_wait(barrier, GROUP - 1 + 2)

    for place, owner in enumerate(ORDER):
        images[t, :, pl.ds(place * SHARE, SHARE)] = img_ref[:, pl.ds(owner * SHARE, SHARE)]

    def image_view(way, s, r):
        return images.at[t - s if way == 0 else t + s, :, pl.ds(r * LANES, LANES)]

    def image_copy(way, s, r):
        view = image_view(way, s, r)
        to = t + 1 if way == 0 else t - 1
        return copy(view, view, ag_send.at[way, s], ag_recv.at[way, s + 1, r], (d, to))

    def gather_step(pair, s, first=False):
        for r in (2 * pair, 2 * pair + 1):
            @pl.when(t >= s)
            def _():
                if not first:
                    arrived(image_view(0, s, r), ag_recv.at[0, s, r])

                @pl.when(t < N_T - 1)
                def _():
                    image_copy(0, s, r).start()

            @pl.when(t + s < N_T)
            def _():
                if not first:
                    arrived(image_view(1, s, r), ag_recv.at[1, s, r])

                @pl.when(t > 0)
                def _():
                    image_copy(1, s, r).start()

    def text_copy(k):
        return copy(txt_ref, texts.at[k], tx_send.at[k], tx_recv.at[k], (lax.rem(d + k, N_DP), t))

    def spread(b, other):
        return copy(
            txt_ref.at[strip(mate(other))], chain_out.at[0, b],
            spread_send, spread_recv, (base + mate(other), t),
        )

    for b in range(STEPS - 1):
        @pl.when(q == GROUP - 1 - b)
        def _():
            for other in range(1, GROUP):
                spread(b, other).start()
            chain_out[0, b] = txt_ref[strip(q), :]

    gather_step(0, 0, True)
    for k in range(1, STEPS):
        @pl.when(q + k < GROUP)
        def _():
            text_copy(k).start()

    def hop_out(h, b):
        return copy(chain_out.at[h, b], chain_out.at[h + 1, b], out_send.at[h], out_recv.at[h + 1, b], up)

    def pass_out(h):
        for b in range(STEPS - 1):
            arrived(chain_out.at[h, b], out_recv.at[h, b])
            hop_out(h, b).start()

    @pl.when(q < GROUP - 3)
    def _():
        arrived(chain_out.at[0], spread_recv)

    @pl.when(q >= GROUP - 3)
    def _():
        arrived(chain_out.at[0, pl.ds(0, 2)], spread_recv)

    for b in range(STEPS - 1):
        hop_out(0, b).start()

    def text_units(k):
        raw = (txt_ref[...] if k == 0 else texts[k]).astype(jnp.float32)
        scales = lax.rsqrt(jnp.sum(raw * raw, axis=1, keepdims=True) + epsilon)
        return raw * scales, scales

    def text_low(k):
        units, _ = text_units(k)
        low[pl.ds(k * SHARE, SHARE), :] = units.astype(jnp.bfloat16)
        low_t[:, pl.ds(k * SHARE, SHARE)] = units.T.astype(jnp.bfloat16)

    text_low(0)
    delta[...] = jnp.zeros_like(delta)
    cross[...] = jnp.zeros_like(cross)
    loss[...] = jnp.zeros_like(loss)

    def first_pair(s, carry):
        pass_out(s)
        gather_step(0, s)
        return carry

    lax.fori_loop(1, N_T, first_pair, 0)
    gather_step(1, 0, True)

    def fan(b, e):
        k = 1 + b + e
        return copy(
            chain_out.at[N_T, b], texts.at[k, strip(q)],
            fan_send.at[b, e], tx_recv.at[k], (base + e, t),
        )

    for b, e in PAIRS:
        if e == 0:
            arrived(chain_out.at[N_T, b], out_recv.at[N_T, b])

        @pl.when(q != e)
        def _():
            fan(b, e).start()

        @pl.when(q == e)
        def _():
            texts[1 + b + e, strip(q), :] = chain_out[N_T, b]

    gather_step(1, 1)

    temper_row = jnp.exp(jnp.full((1, 128), scale_ref[0], jnp.float32))
    temper = temper_row[:, :1]
    bias = bias_ref[0]

    for k in range(1, STEPS):
        @pl.when(q >= k)
        def _():
            arrived(texts.at[k], tx_recv.at[k])

        @pl.when(q < k)
        def _():
            arrived(texts.at[k, pl.ds(0, SHARE - STRIP)], tx_recv.at[k])

        text_low(k)

    def lane_block(owner):
        return pl.ds(pl.multiple_of(owner * SHARE, SHARE), SHARE)

    def compute(r, carry):
        lanes = pl.ds(pl.multiple_of(r * LANES, LANES), LANES)
        raw = images[:, :, lanes].reshape(WIDTH, LANES).astype(jnp.float32)
        scales = lax.rsqrt(jnp.sum(raw * raw, axis=0, keepdims=True) + epsilon)
        unit = (raw * scales).astype(jnp.bfloat16)
        dots = jnp.dot(low[...], unit, preferred_element_type=jnp.float32)
        index = lax.broadcasted_iota(jnp.int32, (STEPS * SHARE, LANES), 0)
        step = index // SHARE
        block = d - step
        block = jnp.where(block < 0, block + N_DP, block)
        names = block * ROWS + t * SHARE + (index - step * SHARE)
        pairs = jnp.concatenate([partner_ref[:, lane_block(N_T - 1 - r)], partner_ref[:, lane_block(r)]], axis=1)
        same = pairs == names
        logits = temper * dots + bias
        z = jnp.where(same, -logits, logits)
        e = jnp.exp(z)
        u = 1.0 + e
        inverse = 1.0 / u
        sigmoid = e * inverse
        terms = jnp.log(u) + (e - (u - 1.0)) * inverse
        grad = jnp.where(same, -sigmoid, sigmoid).astype(jnp.bfloat16)
        along = grad.astype(jnp.float32) * dots
        loss[...] += terms[:, :128] + terms[:, 128:]
        cross[...] += along[:, :128] + along[:, 128:]
        delta[...] += lax.dot_general(
            grad, unit, (((1,), (1,)), ((), ())), preferred_element_type=jnp.float32
        )
        part = jnp.dot(low_t[...], grad, preferred_element_type=jnp.float32)
        back = jnp.sum(along, axis=0, keepdims=True)
        out = ((temper * scales) * (part - unit.astype(jnp.float32) * back)).astype(jnp.bfloat16)
        piece[7 - r] = out[:, :128]
        piece[r] = out[:, 128:]
        return carry

    def sum_rows(m):
        return pl.ds(pl.multiple_of(m * PART, 16), PART)

    def sum_copy(way, owner, m):
        held = from_left if way == 0 else from_right
        to = t + 1 if way == 0 else t - 1
        return copy(
            piece.at[owner, sum_rows(m)], held.at[owner, sum_rows(m)],
            rs_send.at[way, owner], rs_recv.at[way, owner, m], (d, to),
        )

    def sum_take(way, owner, m):
        held = from_left if way == 0 else from_right
        arrived(held.at[owner, sum_rows(m)], rs_recv.at[way, owner, m])
        total = piece[owner, sum_rows(m), :].astype(jnp.float32) + held[owner, sum_rows(m), :].astype(jnp.float32)
        piece[owner, sum_rows(m), :] = total.astype(jnp.bfloat16)

    def reduce_step(p, carry):
        for way in range(2):
            n = p - 2 * (t if way == 0 else N_T - 1 - t)

            @pl.when(jnp.logical_and(n >= 0, n < N_T * PARTS))
            def _():
                a = n // PARTS
                m = n - a * PARTS
                far = jnp.where(a % 2 == 0, N_T - 1 - a // 2, a // 2)
                owner = far if way == 0 else N_T - 1 - far

                @pl.when(owner >= t if way == 0 else owner <= t)
                def _():
                    @pl.when(t > 0 if way == 0 else t < N_T - 1)
                    def _():
                        sum_take(way, owner, m)

                    @pl.when(owner != t)
                    def _():
                        sum_copy(way, owner, m).start()

        return carry

    def second_pair(c, carry):
        compute(c, 0)
        gather_step(1, 2 * c + 2)
        lax.fori_loop(4 * c, 4 * c + 4, reduce_step, 0)
        gather_step(1, 2 * c + 3)
        return carry

    lax.fori_loop(0, 2, second_pair, 0)

    def last_slices(s, carry):
        gather_step(1, s)
        return lax.fori_loop(3 * s - 10, 3 * s - 7, reduce_step, carry)

    lax.fori_loop(6, N_T, last_slices, 0)
    compute(2, 0)
    lax.fori_loop(14, 18, reduce_step, 0)
    compute(3, 0)

    def text_result(k):
        rows = pl.ds(k * SHARE, SHARE)
        units, scales = text_units(k)
        back = jnp.sum(cross[rows, :], axis=1, keepdims=True)
        grads = (temper * scales) * (delta[rows, :] - units * back)
        return grads, jnp.sum(loss[rows, :], axis=1, keepdims=True)

    def grad_copy(k):
        return copy(
            contrib.at[k], returned.at[k], gr_send.at[k], gr_recv.at[k], (lax.rem(d + N_DP - k, N_DP), t)
        )

    def share_copy(k, slot, other):
        return copy(
            contrib.at[k, strip(mate(other))], shares.at[slot],
            share_send.at[k], share_recv, (base + mate(other), t),
        )

    for k in range(STEPS - 1, 0, -1):
        grads, total = text_result(k)
        contrib[k, :, pl.ds(0, WIDTH)] = grads.astype(jnp.bfloat16)
        contrib[k, :, pl.ds(WIDTH, 128)] = jnp.broadcast_to(total, (SHARE, 128)).astype(jnp.bfloat16)

        for slot, (b, e) in enumerate(PAIRS):
            if 1 + b + e == k:
                @pl.when(q == e)
                def _():
                    for other in range(1, GROUP):
                        share_copy(k, slot, other).start()
                    shares[slot] = contrib[k, strip(q), :]

    lax.fori_loop(18, 22, reduce_step, 0)

    def hop_back(h, b):
        return copy(
            chain_back.at[h, b], chain_back.at[h + 1, b], back_send.at[h], back_recv.at[h + 1, b], down
        )

    def pass_back(h):
        for b in range(STEPS - 1):
            arrived(chain_back.at[h, b], back_recv.at[h, b])
            hop_back(h, b).start()

    for e in range(STEPS - 1):
        @pl.when(q == e)
        def _():
            arrived(shares.at[pl.ds(0, STEPS - 1 + e)], share_recv)

    @pl.when(q >= STEPS - 1)
    def _():
        arrived(shares, share_recv)

    for b in range(STEPS - 1):
        total = None
        for slot, (bb, e) in enumerate(PAIRS):
            if bb == b:
                term = shares[slot].astype(jnp.float32)
                total = term if total is None else total + term
        chain_back[0, b] = total.astype(jnp.bfloat16)
        hop_back(0, b).start()

    for k in range(1, STEPS):
        @pl.when(q >= k)
        def _():
            grad_copy(k).start()

    grads, total = text_result(0)
    total = jnp.broadcast_to(total, (SHARE, 128))
    delta[pl.ds(0, SHARE), :] = grads
    loss[pl.ds(0, SHARE), :] = total

    def tail(h, carry):
        pass_back(h)
        return lax.fori_loop(20 + 2 * h, 22 + 2 * h, reduce_step, carry)

    lax.fori_loop(1, N_T, tail, 0)
    lax.fori_loop(36, 40, reduce_step, 0)

    def home(b):
        return copy(
            chain_back.at[N_T, b], returned.at[3, strip(q)],
            home_send.at[b], gr_recv.at[3], (base + GROUP - 1 - b, t),
        )

    for b in range(STEPS - 1):
        arrived(chain_back.at[N_T, b], back_recv.at[N_T, b])

        @pl.when(q != GROUP - 1 - b)
        def _():
            home(b).start()

        @pl.when(q == GROUP - 1 - b)
        def _():
            returned[3, strip(q), :] = chain_back[N_T, b]

    lax.fori_loop(40, WINDOW_STEPS, reduce_step, 0)
    image_out[...] = piece[t].astype(jnp.float32).T.astype(jnp.bfloat16)

    def take(k):
        delta[pl.ds(0, SHARE), :] += returned[k, :, pl.ds(0, WIDTH)].astype(jnp.float32)
        loss[pl.ds(0, SHARE), :] += returned[k, :, pl.ds(WIDTH, 128)].astype(jnp.float32)

    for k in range(1, STEPS - 1):
        @pl.when(q + k < GROUP)
        def _():
            arrived(returned.at[k], gr_recv.at[k])
            take(k)

    @pl.when(q + 3 < GROUP)
    def _():
        arrived(returned.at[3], gr_recv.at[3])

    @pl.when(q + 3 >= GROUP)
    def _():
        arrived(returned.at[3, pl.ds(0, SHARE - STRIP)], gr_recv.at[3])

    take(3)
    text_out[...] = delta[pl.ds(0, SHARE), :].astype(jnp.bfloat16)
    loss_out[...] = loss[pl.ds(0, SHARE), :].T[:1]

    @pl.when(q >= GROUP - 3)
    def _():
        left(txt_ref.at[pl.ds(0, SHARE - STRIP)], spread_send)

    for b, e in PAIRS:
        @pl.when(q != e)
        def _():
            fan(b, e).wait_send()

    for b in range(STEPS - 1):
        @pl.when(q != GROUP - 1 - b)
        def _():
            home(b).wait_send()

    for k in range(1, STEPS):
        @pl.when(q + k < GROUP)
        def _():
            text_copy(k).wait_send()

        @pl.when(q < k)
        def _():
            left(contrib.at[k, pl.ds(0, SHARE - STRIP)], share_send.at[k])

        @pl.when(q >= k)
        def _():
            grad_copy(k).wait_send()

    def drain(s, carry):
        left(chain_out.at[s], out_send.at[s])
        left(chain_back.at[s], back_send.at[s])

        @pl.when(jnp.logical_and(t >= s, t < N_T - 1))
        def _():
            left(images.at[s], ag_send.at[0, s])

        @pl.when(jnp.logical_and(t + s < N_T, t > 0))
        def _():
            left(images.at[s], ag_send.at[1, s])

        @pl.when(s > t)
        def _():
            left(piece.at[s], rs_send.at[0, s])

        @pl.when(s < t)
        def _():
            left(piece.at[s], rs_send.at[1, s])

        return carry

    lax.fori_loop(0, N_T, drain, 0)


def local(image_emb, text_emb, partner, log_scale, logit_bias):
    ordered = image_emb.T
    pairs = partner.reshape(1, ROWS)
    bf16, f32 = jnp.bfloat16, jnp.float32
    dma = pltpu.SemaphoreType.DMA
    vmem = pl.BlockSpec(memory_space=pltpu.VMEM)
    smem = pl.BlockSpec(memory_space=pltpu.SMEM)
    image_grad, text_grad, text_loss = pl.pallas_call(
        kernel,
        name="window_loss",
        out_shape=(
            jax.ShapeDtypeStruct((SHARE, WIDTH), bf16),
            jax.ShapeDtypeStruct((SHARE, WIDTH), bf16),
            jax.ShapeDtypeStruct((1, SHARE), f32),
        ),
        in_specs=[vmem, vmem, vmem, smem, smem],
        out_specs=(vmem, vmem, vmem),
        scratch_shapes=[
            pltpu.VMEM((N_T, SLICE, ROWS), bf16),
            pltpu.VMEM((STEPS, SHARE, WIDTH), bf16),
            pltpu.VMEM((STEPS * SHARE, WIDTH), bf16),
            pltpu.VMEM((WIDTH, STEPS * SHARE), bf16),
            pltpu.VMEM((STEPS * SHARE, WIDTH), f32),
            pltpu.VMEM((STEPS * SHARE, 128), f32),
            pltpu.VMEM((STEPS * SHARE, 128), f32),
            pltpu.VMEM((N_T, WIDTH, SHARE), bf16),
            pltpu.VMEM((N_T, WIDTH, SHARE), bf16),
            pltpu.VMEM((N_T, WIDTH, SHARE), bf16),
            pltpu.VMEM((N_T + 1, STEPS - 1, STRIP, WIDTH), bf16),
            pltpu.VMEM((N_T + 1, STEPS - 1, STRIP, CARRY), bf16),
            pltpu.VMEM((STEPS, SHARE, CARRY), bf16),
            pltpu.VMEM((STEPS, SHARE, CARRY), bf16),
            pltpu.VMEM((len(PAIRS), STRIP, CARRY), bf16),
            dma((2, N_T)), dma((2, N_T + 1, CHUNKS)),
            dma((2, N_T)), dma((2, N_T, PARTS)),
            dma((STEPS,)), dma((STEPS,)), dma, dma,
            dma((N_T,)), dma((N_T + 1, STEPS - 1)), dma((STEPS - 1, STEPS - 1)),
            dma((STEPS,)), dma((STEPS,)), dma((STEPS,)), dma,
            dma((N_T,)), dma((N_T + 1, STEPS - 1)), dma((STEPS - 1,)),
        ],
        compiler_params=pltpu.CompilerParams(
            collective_id=0, has_side_effects=True, vmem_limit_bytes=56 * 2**20
        ),
    )(ordered, text_emb, pairs, log_scale, logit_bias)
    return image_grad, text_grad, text_loss.reshape(SHARE)


def solution(mesh):
    placed = (P("dp", "tensor"), P(("dp", "tensor"), None), P("dp"), P(), P())
    return jax.shard_map(
        local,
        mesh=mesh,
        in_specs=placed,
        out_specs=(P(("dp", "tensor"), None), P(("dp", "tensor"), None), P(("dp", "tensor"))),
        check_vma=False,
    )
```
